512 devices in a mesh: freq: 32 (over x_hi, y, core), rcv: 16 (over x_lo, z).
Axes of the slice: x: 4 (x_hi: 2, x_lo: 2; x = x_hi * 2 + x_lo), y: 8, z: 8, core: 2. Of those that a mesh axis runs over, the one named last changes fastest.
Arguments:
- direct_wave: float32 [32, 2048, 512], P('freq', 'rcv'), may hold values from -6 to 6
- reflection: bfloat16 [2, 64, 2048, 2048], P(None, 'freq', None, 'rcv'), may hold values from -0.0625 to 0.0625
- onset: int32 [32, 2048], P('freq', 'rcv'), may hold values from 64 to 447
Outputs:
- focus_plus: float32 [32, 2048, 512], P('freq', 'rcv')
- focus_minus: float32 [32, 2048, 512], P('freq', 'rcv')
The draws below stay inside these ranges and needn't reach their ends.
All inputs are finite; a program needn't handle non-finite values.
Results may differ from the reference program's by a relative error of at most 0.013.
Values may be sent and summed in bfloat16 or wider, within the bound.
A program may use at most 64 MiB of HBM per device.

```python
import math
import jax
import jax.numpy as jnp
from jax import lax

S = 2048
NF = 64
NT = 512
P_SIZE = 32
ITERS = 2


def with_ends(values, stream_key, low, high):
    longest = values.shape.index(max(values.shape))
    spots = []
    for shift in (0, 1):
        where = [jax.random.randint(jax.random.fold_in(stream_key, axis), (), 0, length) for axis, length in enumerate(values.shape)]
        where[longest] = (where[longest] + shift) % values.shape[longest]
        spots.append(tuple(where))
    return values.at[spots[0]].set(low).at[spots[1]].set(high)


def levels(stream_key, dims, split, low, high):
    factor_of = 1.0
    for position, blocks in split:
        steps = jax.random.uniform(jax.random.fold_in(jax.random.fold_in(stream_key, 6), position), (blocks,), jnp.float32, low / len(split), high / len(split))
        factor_of = factor_of * jnp.repeat(jnp.exp(steps), dims[position] // blocks).reshape((-1,) + (1,) * (len(dims) - 1 - position))
    return factor_of


def gaussian(stream_key, shape, scale, limit, split=(), held_as=jnp.bfloat16):
    entries = jax.random.normal(stream_key, shape, jnp.float32) * scale
    if len(split) > 0:
        entries = levels(stream_key, shape, split, -0.22, 0.18) * entries
    return jnp.clip(entries, min=-limit, max=limit).astype(held_as)


def setup_inputs(seed: int = 0) -> dict:
    streams_of = jax.random.split(jax.random.key(seed), 4)
    return {
        "direct_wave": gaussian(streams_of[0], (P_SIZE, S, NT), 1.0, 6.0, ((0, 32), (1, 16)), jnp.float32),
        "reflection": gaussian(streams_of[1], (2, NF, S, S), (4 * S) ** -0.5, 0.0625, ((1, 32), (3, 16))),
        "onset": with_ends(jax.random.randint(streams_of[2], (P_SIZE, S), NT // 8, 7 * NT // 8), jax.random.fold_in(streams_of[2], 1), NT // 8, (7 * NT // 8) - 1).astype(jnp.int32),
    }


HIGH = lax.Precision.HIGHEST


def tables():
    times = jnp.arange(NT, dtype=jnp.int32)
    bins = jnp.arange(NF, dtype=jnp.int32) + 1
    phase = (times[:, None] * bins[None, :]) % NT
    angle = phase.astype(jnp.float32) * (2.0 * math.pi / NT)
    return jnp.cos(angle), jnp.sin(angle)


def spectrum(field, cosine, sine):
    real_part = jnp.einsum("pst,tk->kps", field, cosine, precision=HIGH)
    imag_part = -jnp.einsum("pst,tk->kps", field, sine, precision=HIGH)
    return jnp.stack([real_part, imag_part]).astype(jnp.bfloat16)


def trace(spec, cosine, sine, window):
    values = spec.astype(jnp.float32)
    field = jnp.einsum("kps,tk->pst", values[0], cosine, precision=HIGH) - jnp.einsum("kps,tk->pst", values[1], sine, precision=HIGH)
    return field * (2.0 / NT) * window


def forward_bin(spec_bin, refl_bin):
    left = spec_bin.astype(jnp.float32)
    right = refl_bin.astype(jnp.float32)
    prods = jnp.einsum("cps,drs->cdpr", left, right, precision=HIGH)
    return jnp.stack([prods[0, 0] - prods[1, 1], prods[0, 1] + prods[1, 0]])


def adjoint_bin(spec_bin, refl_bin):
    left = spec_bin.astype(jnp.float32)
    right = refl_bin.astype(jnp.float32)
    prods = jnp.einsum("cpr,drs->cdps", left, right, precision=HIGH)
    return jnp.stack([prods[0, 0] + prods[1, 1], prods[1, 0] - prods[0, 1]])


def apply_all(func, spec, reflection):
    result = lax.map(lambda w: func(spec[:, w], reflection[:, w]), jnp.arange(NF))
    return jnp.moveaxis(result, 0, 1)


def reference(direct_wave, reflection, onset):
    cosine, sine = tables()
    window = (jnp.arange(NT, dtype=jnp.int32)[None, None, :] < onset[:, :, None]).astype(jnp.float32)
    focus_plus = direct_wave
    focus_minus = jnp.zeros_like(direct_wave)
    for step in range(ITERS):
        upward = apply_all(forward_bin, spectrum(focus_plus, cosine, sine), reflection).astype(jnp.bfloat16)
        focus_minus = trace(upward, cosine, sine, window)
        downward = apply_all(adjoint_bin, spectrum(focus_minus, cosine, sine), reflection).astype(jnp.bfloat16)
        focus_plus = direct_wave + trace(downward, cosine, sine, window)
    return focus_plus, focus_minus
```

```python
import functools
import math

import jax
import jax.numpy as jnp
import ml_dtypes
import numpy as np
from jax import lax
from jax.experimental import pallas as pl
from jax.experimental.pallas import tpu as pltpu
from jax.sharding import PartitionSpec as P

NT = 512
ITERS = 2
BX = 128
F32 = jnp.float32
BF16 = jnp.bfloat16
MESH = pl.DeviceIdType.MESH


def tables(bins):
    phase = np.outer(np.arange(1, bins + 1), np.arange(NT)) % NT
    angle = phase.astype(np.float64) * (2.0 * math.pi / NT)
    rows = np.stack([np.cos(angle), -np.sin(angle)], axis=1).reshape(2 * bins, NT)
    high = rows.astype(ml_dtypes.bfloat16)
    low = (rows - high.astype(np.float64)).astype(ml_dtypes.bfloat16)
    to_bins = np.concatenate([high, low], axis=0)
    scale = ml_dtypes.bfloat16(2.0 / NT)
    to_time = np.concatenate([high.T * scale, low.T * scale], axis=1)
    return to_bins, to_time.astype(ml_dtypes.bfloat16)


def dot(a, b):
    return jnp.dot(a, b, preferred_element_type=F32)


def dot_nt(a, b):
    return lax.dot_general(a, b, (((1,), (1,)), ((), ())), preferred_element_type=F32)


def split(x):
    high = x.astype(BF16)
    return high, (x - high.astype(F32)).astype(BF16)


def kernel(
    nf, nr,
    wave_hbm, refl_hbm, onset_ref, bins_hbm, time_hbm,
    plus_ref, minus_ref,
    wave, refl, to_bins, to_time, first,
    a2a_out, a2a_in, rs_out, rs_in, ag,
    load_sem, a2a_send, a2a_recv, rs_send, rs_recv, ag_send, ag_recv,
):
    me_f = lax.axis_index("freq")
    me_r = lax.axis_index("rcv")
    rows = 4 * nf

    loads = [
        pltpu.make_async_copy(src, dst, load_sem.at[i])
        for i, (src, dst) in enumerate(
            ((wave_hbm.at[0], wave), (bins_hbm, to_bins), (time_hbm, to_time), (refl_hbm, refl))
        )
    ]
    for load in loads:
        load.start()

    barrier = pltpu.get_barrier_semaphore()

    def greet_f(j, _):
        pl.semaphore_signal(
            barrier, inc=1, device_id=(lax.rem(me_f + j, nf), me_r), device_id_type=MESH
        )
        return 0

    def greet_r(j, _):
        pl.semaphore_signal(
            barrier, inc=1, device_id=(me_f, lax.rem(me_r + j, nr)), device_id_type=MESH
        )
        return 0

    lax.fori_loop(1, nf, greet_f, 0)
    lax.fori_loop(1, nr, greet_r, 0)

    n_ids = lax.broadcasted_iota(jnp.int32, (rows, BX), 0)
    is_im = (n_ids % 2) == 1
    second = ((n_ids // 2) % 2) == 1
    onset = onset_ref[...]
    early = lax.broadcasted_iota(jnp.int32, (NT, BX), 0) < onset

    def exchange(stage, value):
        out, into = a2a_out.at[stage], a2a_in.at[stage]
        out[...] = value.reshape(nf, 4, BX)

        def push(j, _):
            to = lax.rem(me_f + j, nf)
            pltpu.make_async_remote_copy(
                src_ref=out.at[to], dst_ref=into.at[me_f],
                send_sem=a2a_send.at[stage], recv_sem=a2a_recv.at[stage],
                device_id=(to, me_r), device_id_type=MESH,
            ).start()
            return 0

        lax.fori_loop(1, nf, push, 0)
        pltpu.make_async_copy(out.at[me_f], into.at[me_f], a2a_recv.at[stage]).start()
        pltpu.make_async_copy(into, into, a2a_recv.at[stage]).wait()
        return into[...].reshape(rows, BX)

    def spectrum(field):
        high, low = split(field)
        both = dot(to_bins[...], high)
        return both[:rows] + both[rows:] + dot(to_bins[:rows], low)

    def trace(spec):
        both = jnp.concatenate([spec, spec], axis=0)
        return jnp.where(early, dot(to_time[...], both), 0.0)

    def turn(x):
        return jnp.where(is_im, jnp.roll(x, 1, axis=0), -jnp.roll(x, -1, axis=0))

    def forward(it, spec):
        spec = spec.astype(BF16).astype(F32)
        turned = turn(spec)
        weights = jnp.concatenate(
            [
                jnp.where(second, 0.0, spec), jnp.where(second, 0.0, turned),
                jnp.where(second, spec, 0.0), jnp.where(second, turned, 0.0),
            ],
            axis=1,
        ).astype(BF16)
        half = max(nr // 2, 1) * BX
        for part in range(nr * BX // half):
            rows_of = pl.ds(part * half, half)
            left = jnp.concatenate([refl[c, w, rows_of, :] for w in range(2) for c in range(2)], axis=1)
            block = dot_nt(left, weights).astype(BF16)
            rs_out[it, pl.ds(part * half // BX, half // BX)] = block.reshape(half // BX, BX, rows)

        def push(j, _):
            to = lax.rem(me_r + j, nr)
            pltpu.make_async_remote_copy(
                src_ref=rs_out.at[it, to], dst_ref=rs_in.at[it, me_r],
                send_sem=rs_send.at[it], recv_sem=rs_recv.at[it],
                device_id=(me_f, to), device_id_type=MESH,
            ).start()
            return 0

        lax.fori_loop(1, nr, push, 0)
        pltpu.make_async_copy(rs_out.at[it, me_r], rs_in.at[it, me_r], rs_recv.at[it]).start()
        pltpu.make_async_copy(rs_in.at[it], rs_in.at[it], rs_recv.at[it]).wait()
        total = rs_in[it, 0].astype(F32)
        for j in range(1, nr):
            total = total + rs_in[it, j].astype(F32)
        return total.T

    def adjoint(it, spec):
        ag[it, me_r] = spec.astype(BF16)

        def push(j, _):
            to = lax.rem(me_r + j, nr)
            pltpu.make_async_remote_copy(
                src_ref=ag.at[it, me_r], dst_ref=ag.at[it, me_r],
                send_sem=ag_send.at[it], recv_sem=ag_recv.at[it],
                device_id=(me_f, to), device_id_type=MESH,
            ).start()
            return 0

        lax.fori_loop(1, nr, push, 0)
        others = ag.at[it, pl.ds(0, nr - 1)]
        pltpu.make_async_copy(others, others, ag_recv.at[it]).wait()
        left = jnp.concatenate([ag[it, j] for j in range(nr)], axis=1)
        products = [
            dot(left, jnp.concatenate([refl[0, w], refl[1, w]], axis=1)) for w in range(2)
        ]
        product = jnp.where(
            jnp.concatenate([second, second], axis=1), products[1], products[0]
        )
        return product[:, :BX] - turn(product[:, BX:])

    loads[0].wait()
    loads[1].wait()
    high, low = split(wave[...])
    both = dot_nt(to_bins[...], high)
    first[...] = both[:rows] + both[rows:] + dot_nt(to_bins[:rows], low)
    loads[2].wait()

    pl.semaphore_wait(barrier, nf + nr - 2)
    onset_col = jnp.broadcast_to(onset, (BX, BX)).T

    def finish(spec):
        both = jnp.concatenate([spec.T, spec.T], axis=1).astype(BF16)
        field = dot(both, to_bins[...]) * (2.0 / NT)
        samples = lax.broadcasted_iota(jnp.int32, (BX, BX), 1)
        return [
            jnp.where(samples + k * BX < onset_col, field[:, k * BX:(k + 1) * BX], 0.0)
            for k in range(NT // BX)
        ]

    plus_spec = first[...]
    for it in range(ITERS):
        plus_bins = exchange(4 * it, plus_spec)
        if it == 0:
            loads[3].wait()
        upward = exchange(4 * it + 1, forward(it, plus_bins)).astype(BF16)
        minus_bins = exchange(4 * it + 2, spectrum(trace(upward)))
        if it == ITERS - 1:
            for k, part in enumerate(finish(upward.astype(F32))):
                minus_ref[0, :, pl.ds(k * BX, BX)] = part
        downward = exchange(4 * it + 3, adjoint(it, minus_bins)).astype(BF16)
        if it < ITERS - 1:
            plus_spec = first[...] + spectrum(trace(downward))
        else:
            for k, part in enumerate(finish(downward.astype(F32))):
                span = pl.ds(k * BX, BX)
                plus_ref[0, :, span] = wave[:, span] + part

    for stage in range(4 * ITERS):
        sent = a2a_out.at[stage, pl.ds(0, nf - 1)]
        pltpu.make_async_copy(sent, sent, a2a_send.at[stage]).wait()
    for it in range(ITERS):
        sent = rs_out.at[it, pl.ds(0, nr - 1)]
        pltpu.make_async_copy(sent, sent, rs_send.at[it]).wait()
        sent = ag.at[it, pl.ds(0, nr - 1)]
        pltpu.make_async_copy(sent, sent, ag_send.at[it]).wait()


def solution(mesh):
    nf, nr = mesh.shape["freq"], mesh.shape["rcv"]
    rows = 4 * nf
    to_bins, to_time = tables(2 * nf)

    def shards(direct_wave, reflection, onset):
        out = jax.ShapeDtypeStruct(direct_wave.shape, F32)
        anywhere = pl.BlockSpec(memory_space=pl.ANY)
        vmem = pl.BlockSpec(memory_space=pltpu.VMEM)
        return pl.pallas_call(
            functools.partial(kernel, nf, nr),
            out_shape=(out, out),
            in_specs=[anywhere, anywhere, vmem, anywhere, anywhere],
            out_specs=(vmem, vmem),
            scratch_shapes=[
                pltpu.VMEM(direct_wave.shape[1:], F32),
                pltpu.VMEM(reflection.shape, BF16),
                pltpu.VMEM(to_bins.shape, BF16),
                pltpu.VMEM(to_time.shape, BF16),
                pltpu.VMEM((rows, BX), F32),
                pltpu.VMEM((4 * ITERS, nf, 4, BX), F32),
                pltpu.VMEM((4 * ITERS, nf, 4, BX), F32),
                pltpu.VMEM((ITERS, nr, BX, rows), BF16),
                pltpu.VMEM((ITERS, nr, BX, rows), BF16),
                pltpu.VMEM((ITERS, nr, rows, BX), BF16),
                pltpu.SemaphoreType.DMA((4,)),
                pltpu.SemaphoreType.DMA((4 * ITERS,)),
                pltpu.SemaphoreType.DMA((4 * ITERS,)),
                pltpu.SemaphoreType.DMA((ITERS,)),
                pltpu.SemaphoreType.DMA((ITERS,)),
                pltpu.SemaphoreType.DMA((ITERS,)),
                pltpu.SemaphoreType.DMA((ITERS,)),
            ],
            compiler_params=pltpu.CompilerParams(
                collective_id=0, has_side_effects=True, vmem_limit_bytes=32 * 2**20
            ),
        )(direct_wave, reflection, onset, jnp.asarray(to_bins), jnp.asarray(to_time))

    return jax.shard_map(
        shards,
        mesh=mesh,
        in_specs=(P("freq", "rcv", None), P(None, "freq", None, "rcv"), P("freq", "rcv")),
        out_specs=(P("freq", "rcv", None), P("freq", "rcv", None)),
        check_vma=False,
    )
```

```python
import functools
import math

import jax
import jax.numpy as jnp
import ml_dtypes
import numpy as np
from jax import lax
from jax.experimental import pallas as pl
from jax.experimental.pallas import tpu as pltpu
from jax.sharding import PartitionSpec as P

NT = 512
ITERS = 2
BX = 128
GROUPS = 4
SUM_STRAIGHT = (0, 3)
GATHER_STRAIGHT = (3,)
SUM_ORDER = (0, 3, 1, 2)
GATHER_ORDER = (3, 0, 1, 2)
F32 = jnp.float32
BF16 = jnp.bfloat16
MESH = pl.DeviceIdType.MESH


def tables(bins):
    phase = np.outer(np.arange(1, bins + 1), np.arange(NT)) % NT
    angle = phase.astype(np.float64) * (2.0 * math.pi / NT)
    rows = np.stack([np.cos(angle), -np.sin(angle)], axis=1).reshape(2 * bins, NT)
    high = rows.astype(ml_dtypes.bfloat16)
    low = (rows - high.astype(np.float64)).astype(ml_dtypes.bfloat16)
    to_bins = np.concatenate([high, low], axis=0)
    scale = ml_dtypes.bfloat16(2.0 / NT)
    to_time = np.concatenate([high.T * scale, low.T * scale], axis=1)
    return to_bins, to_time.astype(ml_dtypes.bfloat16)


def dot(a, b):
    return jnp.dot(a, b, preferred_element_type=F32)


def dot_nt(a, b):
    return lax.dot_general(a, b, (((1,), (1,)), ((), ())), preferred_element_type=F32)


def split(x):
    high = x.astype(BF16)
    return high, (x - high.astype(F32)).astype(BF16)


def ring(n, k):
    return min(k % n, -k % n)


def offsets_freq(ny):
    steps = [(h, y, c) for h in range(2) for y in range(ny) for c in range(2)]
    return sorted(steps, key=lambda s: (ring(ny, s[1]) + 2 * s[0], -s[0], s[1], s[2]))


def offsets_rcv(nz):
    steps = [(h, z) for h in range(2) for z in range(nz)][1:]
    return sorted(steps, key=lambda s: (-ring(nz, s[1]) - s[0], s))


def kernel(
    nf, nr,
    wave_hbm, refl_hbm, onset_hbm, bins_hbm, time_hbm,
    plus_ref, minus_ref,
    wave, refl, onset_ref, turned_refl, to_bins, to_time, first,
    a2a_out, a2a_in, rs_out, rs_mate, rs_pair, rs_in, ag,
    load_sem, bins_send, bins_recv, time_send, time_recv, rs_send, rs_recv, ag_send, ag_recv,
    mate_send, mate_recv, relay_send, relay_recv,
):
    me_f = lax.axis_index("freq")
    me_r = lax.axis_index("rcv")
    rows = 4 * nf
    ny, nz = nf // 4, nr // 2
    near = offsets_freq(ny)
    back = [near.index((h, -y % ny, c)) for h, y, c in near]
    size = nf // GROUPS
    deep = 4 * size

    half, y_at, core = me_f // (2 * ny), (me_f // 2) % ny, me_f % 2
    freq_at = [
        (((half + h) % 2) * ny + (y_at + y) % ny) * 2 + (core + c) % 2 for h, y, c in near
    ]
    side, z_at = me_r // nz, me_r % nz
    rcv_at = [((side + h) % 2) * nz + (z_at + z) % nz for h, z in offsets_rcv(nz)]
    line_at = [side * nz + (z_at + z) % nz for h, z in offsets_rcv(nz) if h == 0]
    mate = (1 - side) * nz + z_at
    ours, theirs = pl.ds(side * nz, nz), pl.ds((1 - side) * nz, nz)

    loads = [
        pltpu.make_async_copy(src, dst, load_sem.at[i])
        for i, (src, dst) in enumerate(
            (
                (wave_hbm.at[0], wave), (bins_hbm, to_bins), (time_hbm, to_time),
                (refl_hbm, refl), (onset_hbm, onset_ref),
            )
        )
    ]
    for load in loads:
        load.start()

    barrier = pltpu.get_barrier_semaphore()
    for j in range(nf - 1, 0, -1):
        pl.semaphore_signal(barrier, inc=1, device_id=(freq_at[j], me_r), device_id_type=MESH)
    for to in rcv_at:
        pl.semaphore_signal(barrier, inc=1, device_id=(me_f, to), device_id_type=MESH)

    is_im = (lax.broadcasted_iota(jnp.int32, (rows, BX), 0) % 2) == 1
    second = ((lax.broadcasted_iota(jnp.int32, (rows, BX), 0) // 2) % 2) == 1
    group_im, group_second = is_im[:deep], second[:deep]
    def wait(ref, sem):
        pltpu.make_async_copy(ref, ref, sem).wait()

    def to_bin_owners(it, part, value):
        stage = 4 * it + 2 * part
        out, into = a2a_out.at[stage], a2a_in.at[stage]
        out[...] = value.reshape(nf, 4, BX)
        for j in range(nf - 1, 0, -1):
            pltpu.make_async_remote_copy(
                src_ref=out.at[freq_at[j]], dst_ref=into.at[back[j]],
                send_sem=bins_send.at[it, part], recv_sem=bins_recv.at[it, part, back[j] // size],
                device_id=(freq_at[j], me_r), device_id_type=MESH,
            ).start()
        into[0] = out[me_f]

    def from_time_owners(it, part, g):
        stage, least = 4 * it + 2 * part, 1 if g == 0 else 0
        if size > least:
            wait(
                a2a_in.at[stage, pl.ds(g * size + least, size - least)], bins_recv.at[it, part, g]
            )
        return a2a_in[stage, pl.ds(g * size, size)].reshape(deep, BX)

    def to_time_owners(it, part, g, value):
        stage = 4 * it + 2 * part + 1
        out, into = a2a_out.at[stage], a2a_in.at[stage]
        out[pl.ds(g * size, size)] = value.reshape(size, 4, BX)
        for j in range((g + 1) * size - 1, max(g * size, 1) - 1, -1):
            pltpu.make_async_remote_copy(
                src_ref=out.at[j], dst_ref=into.at[me_f],
                send_sem=time_send.at[it, part], recv_sem=time_recv.at[it, part],
                device_id=(freq_at[j], me_r), device_id_type=MESH,
            ).start()
        if g == 0:
            into[me_f] = out[0]

    def from_bin_owners(it, part):
        stage = 4 * it + 2 * part + 1
        wait(a2a_in.at[stage, pl.ds(0, nf - 1)], time_recv.at[it, part])
        return a2a_in[stage].reshape(rows, BX).astype(BF16)

    def spectrum(field):
        high, low = split(field)
        both = dot(to_bins[...], high)
        return both[:rows] + both[rows:] + dot(to_bins[:rows], low)

    def trace(spec):
        both = jnp.concatenate([spec, spec], axis=0)
        return jnp.where(early, dot(to_time[...], both), 0.0)

    def turn(x):
        return jnp.where(group_im, jnp.roll(x, 1, axis=0), -jnp.roll(x, -1, axis=0))

    def forward(it, g, spec):
        spec = spec.astype(BF16).astype(F32)
        turned = turn(spec)
        weights = jnp.concatenate(
            [
                jnp.where(group_second, 0.0, spec), jnp.where(group_second, 0.0, turned),
                jnp.where(group_second, spec, 0.0), jnp.where(group_second, turned, 0.0),
            ],
            axis=1,
        ).astype(BF16)
        for k in range(nr // 2):
            pair = dot(weights, turned_refl[:, pl.ds(2 * k * BX, 2 * BX)]).astype(BF16)
            rs_out[it, g, 2 * k] = pair[:, :BX]
            rs_out[it, g, 2 * k + 1] = pair[:, BX:]
        if g not in SUM_STRAIGHT:
            pltpu.make_async_remote_copy(
                src_ref=rs_out.at[it, g, theirs], dst_ref=rs_mate.at[it, g],
                send_sem=mate_send.at[it, g], recv_sem=mate_recv.at[it, g],
                device_id=(me_f, mate), device_id_type=MESH,
            ).start()
            return
        for j, to in enumerate(rcv_at):
            pltpu.make_async_remote_copy(
                src_ref=rs_out.at[it, g, to], dst_ref=rs_in.at[it, g, j],
                send_sem=rs_send.at[it, g], recv_sem=rs_recv.at[it, g],
                device_id=(me_f, to), device_id_type=MESH,
            ).start()

    def paired(it, g):
        wait(rs_mate.at[it, g], mate_recv.at[it, g])
        both = rs_out[it, g, ours].astype(F32) + rs_mate[it, g].astype(F32)
        rs_pair[it, g] = both.astype(BF16)
        for j, to in enumerate(line_at):
            pltpu.make_async_remote_copy(
                src_ref=rs_pair.at[it, g, to % nz], dst_ref=rs_in.at[it, g, j],
                send_sem=rs_send.at[it, g], recv_sem=rs_recv.at[it, g],
                device_id=(me_f, to), device_id_type=MESH,
            ).start()

    def summed(it, g):
        if g in SUM_STRAIGHT:
            terms, total = nr - 1, rs_out[it, g, me_r].astype(F32)
        else:
            terms, total = nz - 1, rs_pair[it, g, z_at].astype(F32)
        if terms:
            wait(rs_in.at[it, g, pl.ds(0, terms)], rs_recv.at[it, g])
        for j in range(terms):
            total = total + rs_in[it, g, j].astype(F32)
        return total

    def gather(it, g, spec):
        ag[it, g, me_r] = spec.astype(BF16)
        for to in rcv_at if g in GATHER_STRAIGHT else line_at:
            pltpu.make_async_remote_copy(
                src_ref=ag.at[it, g, me_r], dst_ref=ag.at[it, g, me_r],
                send_sem=ag_send.at[it, g], recv_sem=ag_recv.at[it, g],
                device_id=(me_f, to), device_id_type=MESH,
            ).start()

    def relay(it, g):
        if nz > 1:
            wait(ag.at[it, g, pl.ds(0, nz - 1)], ag_recv.at[it, g])
        pltpu.make_async_remote_copy(
            src_ref=ag.at[it, g, ours], dst_ref=ag.at[it, g, ours],
            send_sem=relay_send.at[it, g], recv_sem=relay_recv.at[it, g],
            device_id=(me_f, mate), device_id_type=MESH,
        ).start()

    def adjoint(it, g):
        if g in GATHER_STRAIGHT:
            wait(ag.at[it, g, pl.ds(0, nr - 1)], ag_recv.at[it, g])
        else:
            wait(ag.at[it, g, pl.ds(0, nz)], relay_recv.at[it, g])
        left = jnp.concatenate([ag[it, g, j] for j in range(nr)], axis=1)
        one, two = [dot(left, jnp.concatenate([refl[0, w], refl[1, w]], axis=1)) for w in range(2)]
        by_re = jnp.where(group_second, two[:, :BX], one[:, :BX])
        by_im = jnp.where(group_second, two[:, BX:], one[:, BX:])
        return by_re - turn(by_im)

    loads[0].wait()
    loads[1].wait()
    high, low = split(wave[...])
    both = dot_nt(to_bins[...], high)
    first[...] = both[:rows] + both[rows:] + dot_nt(to_bins[:rows], low)
    loads[2].wait()
    loads[4].wait()
    onset = onset_ref[...]
    early = lax.broadcasted_iota(jnp.int32, (NT, BX), 0) < onset
    onset_col = jnp.broadcast_to(onset, (BX, BX)).T

    def finish(spec):
        both = jnp.concatenate([spec.T, spec.T], axis=1).astype(BF16)
        field = dot(both, to_bins[...]) * (2.0 / NT)
        samples = lax.broadcasted_iota(jnp.int32, (BX, BX), 1)
        return [
            jnp.where(samples + k * BX < onset_col, field[:, k * BX:(k + 1) * BX], 0.0)
            for k in range(NT // BX)
        ]

    pl.semaphore_wait(barrier, nf + nr - 2)
    to_bin_owners(0, 0, first[...])
    loads[3].wait()
    for w in range(2):
        for c in range(2):
            for k in range(nr):
                block = refl[c, w, pl.ds(k * BX, BX), :]
                turned_refl[pl.ds((2 * w + c) * BX, BX), pl.ds(k * BX, BX)] = block.T
    for it in range(ITERS):
        for g in range(GROUPS):
            forward(it, g, from_time_owners(it, 0, g))
        for g in range(GROUPS):
            if g not in SUM_STRAIGHT:
                paired(it, g)
        for g in SUM_ORDER:
            to_time_owners(it, 0, g, summed(it, g))
        upward = from_bin_owners(it, 0)
        to_bin_owners(it, 1, spectrum(trace(upward)))
        if it == ITERS - 1:
            for k, part in enumerate(finish(upward.astype(F32))):
                minus_ref[0, :, pl.ds(k * BX, BX)] = part
        for g in range(GROUPS):
            gather(it, g, from_time_owners(it, 1, g))
        for g in range(GROUPS):
            if g not in GATHER_STRAIGHT:
                relay(it, g)
        for g in GATHER_ORDER:
            to_time_owners(it, 1, g, adjoint(it, g))
        downward = from_bin_owners(it, 1)
        if it < ITERS - 1:
            to_bin_owners(it + 1, 0, first[...] + spectrum(trace(downward)))
        else:
            for k, part in enumerate(finish(downward.astype(F32))):
                span = pl.ds(k * BX, BX)
                plus_ref[0, :, span] = wave[:, span] + part

    for it in range(ITERS):
        for part in range(2):
            stage = 4 * it + 2 * part
            wait(a2a_out.at[stage, pl.ds(0, nf - 1)], bins_send.at[it, part])
            wait(a2a_out.at[stage + 1, pl.ds(0, nf - 1)], time_send.at[it, part])
        for g in range(GROUPS):
            if g in SUM_STRAIGHT:
                wait(rs_out.at[it, g, pl.ds(0, nr - 1)], rs_send.at[it, g])
            else:
                wait(rs_out.at[it, g, theirs], mate_send.at[it, g])
                if nz > 1:
                    wait(rs_pair.at[it, g, pl.ds(0, nz - 1)], rs_send.at[it, g])
            if g in GATHER_STRAIGHT:
                wait(ag.at[it, g, pl.ds(0, nr - 1)], ag_send.at[it, g])
            else:
                wait(ag.at[it, g, ours], relay_send.at[it, g])
                if nz > 1:
                    wait(ag.at[it, g, pl.ds(0, nz - 1)], ag_send.at[it, g])


def solution(mesh):
    nf, nr = mesh.shape["freq"], mesh.shape["rcv"]
    rows, deep = 4 * nf, 4 * nf // GROUPS
    to_bins, to_time = tables(2 * nf)

    def shards(direct_wave, reflection, onset):
        out = pltpu.VMEM(direct_wave.shape, F32)
        in_hbm = [
            pltpu.with_memory_space_constraint(array, pltpu.HBM)
            for array in (direct_wave, reflection, onset, jnp.asarray(to_bins), jnp.asarray(to_time))
        ]
        anywhere = pl.BlockSpec(memory_space=pl.ANY)
        vmem = pl.BlockSpec(memory_space=pltpu.VMEM)
        dma = pltpu.SemaphoreType.DMA
        return pl.pallas_call(
            functools.partial(kernel, nf, nr),
            out_shape=(out, out),
            in_specs=[anywhere] * 5,
            out_specs=(vmem, vmem),
            scratch_shapes=[
                pltpu.VMEM(direct_wave.shape[1:], F32),
                pltpu.VMEM(reflection.shape, BF16),
                pltpu.VMEM(onset.shape, jnp.int32),
                pltpu.VMEM((4 * BX, nr * BX), BF16),
                pltpu.VMEM(to_bins.shape, BF16),
                pltpu.VMEM(to_time.shape, BF16),
                pltpu.VMEM((rows, BX), F32),
                pltpu.VMEM((4 * ITERS, nf, 4, BX), F32),
                pltpu.VMEM((4 * ITERS, nf, 4, BX), F32),
                pltpu.VMEM((ITERS, GROUPS, nr, deep, BX), BF16),
                pltpu.VMEM((ITERS, GROUPS, nr // 2, deep, BX), BF16),
                pltpu.VMEM((ITERS, GROUPS, nr // 2, deep, BX), BF16),
                pltpu.VMEM((ITERS, GROUPS, nr - 1, deep, BX), BF16),
                pltpu.VMEM((ITERS, GROUPS, nr, deep, BX), BF16),
                dma((5,)),
                dma((ITERS, 2)),
                dma((ITERS, 2, GROUPS)),
                dma((ITERS, 2)),
                dma((ITERS, 2)),
            ]
            + [dma((ITERS, GROUPS))] * 8,
            compiler_params=pltpu.CompilerParams(
                collective_id=0, has_side_effects=True, vmem_limit_bytes=32 * 2**20
            ),
        )(*in_hbm)

    return jax.shard_map(
        shards,
        mesh=mesh,
        in_specs=(P("freq", "rcv", None), P(None, "freq", None, "rcv"), P("freq", "rcv")),
        out_specs=(P("freq", "rcv", None), P("freq", "rcv", None)),
        check_vma=False,
    )
```

```python
import functools
import math

import jax
import jax.numpy as jnp
import ml_dtypes
import numpy as np
from jax import lax
from jax.experimental import pallas as pl
from jax.experimental.pallas import tpu as pltpu
from jax.sharding import PartitionSpec as P

NT = 512
ITERS = 2
BX = 128
GROUPS = 4
SUM_STRAIGHT = (0, 3)
GATHER_STRAIGHT = (3,)
SUM_ORDER = (0, 3, 1, 2)
GATHER_SETS = ((3,), (0, 1, 2))
F32 = jnp.float32
BF16 = jnp.bfloat16
MESH = pl.DeviceIdType.MESH


def tables(bins):
    phase = np.outer(np.arange(1, bins + 1), np.arange(NT)) % NT
    angle = phase.astype(np.float64) * (2.0 * math.pi / NT)
    rows = np.stack([np.cos(angle), -np.sin(angle)], axis=1).reshape(2 * bins, NT)
    high = rows.astype(ml_dtypes.bfloat16)
    low = (rows - high.astype(np.float64)).astype(ml_dtypes.bfloat16)
    to_bins = np.concatenate([high, low], axis=0)
    scale = ml_dtypes.bfloat16(2.0 / NT)
    to_time = np.concatenate([high.T * scale, low.T * scale], axis=1)
    return to_bins, to_time.astype(ml_dtypes.bfloat16)


def dot(a, b):
    return jnp.dot(a, b, preferred_element_type=F32)


def dot_nt(a, b):
    return lax.dot_general(a, b, (((1,), (1,)), ((), ())), preferred_element_type=F32)


def split(x):
    high = x.astype(BF16)
    return high, (x - high.astype(F32)).astype(BF16)


def ring(n, k):
    return min(k % n, -k % n)


def offsets_freq(ny):
    steps = [(h, y, c) for h in range(2) for y in range(ny) for c in range(2)]
    return sorted(steps, key=lambda s: (ring(ny, s[1]) + 2 * s[0], -s[0], s[1], s[2]))


def offsets_rcv(nz):
    steps = [(h, z) for h in range(2) for z in range(nz)][1:]
    return sorted(steps, key=lambda s: (-ring(nz, s[1]) - s[0], s))


def kernel(
    nf, nr,
    wave_hbm, refl_hbm, onset_hbm, bins_hbm, time_hbm,
    plus_ref, minus_ref,
    wave, refl, onset_ref, turned_refl, to_bins, to_time, first,
    a2a_out, a2a_in, rs_out, rs_mate, rs_pair, rs_in, ag,
    load_sem, bins_send, bins_recv, time_send, time_recv, rs_send, rs_recv, ag_send, ag_recv,
    mate_send, mate_recv, relay_send, relay_recv,
):
    me_f = lax.axis_index("freq")
    me_r = lax.axis_index("rcv")
    rows = 4 * nf
    ny, nz = nf // 4, nr // 2
    near = offsets_freq(ny)
    back = [near.index((h, -y % ny, c)) for h, y, c in near]
    size = nf // GROUPS
    deep = 4 * size

    last = nf - max(size * GROUPS // 4, 1)
    issue_order = [*range(nf - 1, last - 1, -1), *range(1, last)]

    half, y_at, core = me_f // (2 * ny), (me_f // 2) % ny, me_f % 2
    freq_at = [
        (((half + h) % 2) * ny + (y_at + y) % ny) * 2 + (core + c) % 2 for h, y, c in near
    ]
    side, z_at = me_r // nz, me_r % nz
    rcv_at = [(h, (side + h) % 2 * nz + (z_at + z) % nz) for h, z in offsets_rcv(nz)]
    line_at = [to for h, to in rcv_at if h == 0]
    mate = (1 - side) * nz + z_at
    ours, theirs = pl.ds(side * nz, nz), pl.ds((1 - side) * nz, nz)

    loads = [
        pltpu.make_async_copy(src, dst, load_sem.at[i])
        for i, (src, dst) in enumerate(
            (
                (wave_hbm.at[0], wave), (bins_hbm, to_bins), (time_hbm, to_time),
                (refl_hbm, refl), (onset_hbm, onset_ref),
            )
        )
    ]
    for load in loads:
        load.start()

    barrier = pltpu.get_barrier_semaphore()
    peers = [(ring(ny, near[j][1]) + 2 * near[j][0], freq_at[j], me_r) for j in range(1, nf)]
    peers += [
        (ring(nz, z) + h, me_f, to) for (h, z), (_, to) in zip(offsets_rcv(nz), rcv_at)
    ]
    for _, f, r in sorted(peers, key=lambda peer: -peer[0]):
        pl.semaphore_signal(barrier, inc=1, device_id=(f, r), device_id_type=MESH)

    is_im = (lax.broadcasted_iota(jnp.int32, (rows, BX), 0) % 2) == 1
    second = ((lax.broadcasted_iota(jnp.int32, (rows, BX), 0) // 2) % 2) == 1
    group_second = second[:deep]
    def wait(ref, sem):
        pltpu.make_async_copy(ref, ref, sem).wait()

    def to_bin_owners(it, part, value):
        stage = 4 * it + 2 * part
        out, into = a2a_out.at[stage], a2a_in.at[stage]
        out[...] = value.reshape(nf, 4, BX)
        for j in issue_order:
            pltpu.make_async_remote_copy(
                src_ref=out.at[freq_at[j]], dst_ref=into.at[back[j]],
                send_sem=bins_send.at[it, part], recv_sem=bins_recv.at[it, part, back[j] // size],
                device_id=(freq_at[j], me_r), device_id_type=MESH,
            ).start()
        into[0] = out[me_f]

    def from_time_owners(it, part, g):
        stage, least = 4 * it + 2 * part, 1 if g == 0 else 0
        if size > least:
            wait(
                a2a_in.at[stage, pl.ds(g * size + least, size - least)], bins_recv.at[it, part, g]
            )
        return a2a_in[stage, pl.ds(g * size, size)].reshape(deep, BX)

    def to_time_owners(it, part, g, value):
        stage = 4 * it + 2 * part + 1
        out, into = a2a_out.at[stage], a2a_in.at[stage]
        out[pl.ds(g * size, size)] = value.reshape(size, 4, BX)
        for j in range((g + 1) * size - 1, max(g * size, 1) - 1, -1):
            pltpu.make_async_remote_copy(
                src_ref=out.at[j], dst_ref=into.at[me_f],
                send_sem=time_send.at[it, part], recv_sem=time_recv.at[it, part],
                device_id=(freq_at[j], me_r), device_id_type=MESH,
            ).start()
        if g == 0:
            into[me_f] = out[0]

    def from_bin_owners(it, part):
        stage = 4 * it + 2 * part + 1
        wait(a2a_in.at[stage, pl.ds(0, nf - 1)], time_recv.at[it, part])
        return a2a_in[stage].reshape(rows, BX).astype(BF16)

    def spectrum(field):
        high, low = split(field)
        both = dot(to_bins[...], high)
        return both[:rows] + both[rows:] + dot(to_bins[:rows], low)

    def trace(spec):
        both = jnp.concatenate([spec, spec], axis=0)
        return jnp.where(early, dot(to_time[...], both), 0.0)

    def turn(x):
        return jnp.where(is_im[:x.shape[0]], jnp.roll(x, 1, axis=0), -jnp.roll(x, -1, axis=0))

    def forward(it, g, spec):
        spec = spec.astype(BF16).astype(F32)
        turned = turn(spec)
        weights = jnp.concatenate(
            [
                jnp.where(group_second, 0.0, spec), jnp.where(group_second, 0.0, turned),
                jnp.where(group_second, spec, 0.0), jnp.where(group_second, turned, 0.0),
            ],
            axis=1,
        ).astype(BF16)
        for part in (1 - side, side):
            for k in range(nz // 2):
                at = part * nz + 2 * k
                columns = pl.ds(pl.multiple_of(at * BX, 2 * BX), 2 * BX)
                pair = dot(weights, turned_refl[:, columns]).astype(BF16)
                rs_out[it, g, at] = pair[:, :BX]
                rs_out[it, g, at + 1] = pair[:, BX:]
            if g in SUM_STRAIGHT:
                for j, (h, to) in enumerate(rcv_at):
                    if (h == 0) == (part is side):
                        pltpu.make_async_remote_copy(
                            src_ref=rs_out.at[it, g, to], dst_ref=rs_in.at[it, g, j],
                            send_sem=rs_send.at[it, g], recv_sem=rs_recv.at[it, g],
                            device_id=(me_f, to), device_id_type=MESH,
                        ).start()
            elif part is not side:
                pltpu.make_async_remote_copy(
                    src_ref=rs_out.at[it, g, theirs], dst_ref=rs_mate.at[it, g],
                    send_sem=mate_send.at[it, g], recv_sem=mate_recv.at[it, g],
                    device_id=(me_f, mate), device_id_type=MESH,
                ).start()

    def paired(it, g):
        wait(rs_mate.at[it, g], mate_recv.at[it, g])
        both = rs_out[it, g, ours].astype(F32) + rs_mate[it, g].astype(F32)
        rs_pair[it, g] = both.astype(BF16)
        for j, to in enumerate(line_at):
            pltpu.make_async_remote_copy(
                src_ref=rs_pair.at[it, g, to % nz], dst_ref=rs_in.at[it, g, j],
                send_sem=rs_send.at[it, g], recv_sem=rs_recv.at[it, g],
                device_id=(me_f, to), device_id_type=MESH,
            ).start()

    def summed(it, g):
        if g in SUM_STRAIGHT:
            terms, total = nr - 1, rs_out[it, g, me_r].astype(F32)
        else:
            terms, total = nz - 1, rs_pair[it, g, z_at].astype(F32)
        if terms:
            wait(rs_in.at[it, g, pl.ds(0, terms)], rs_recv.at[it, g])
        for j in range(terms):
            total = total + rs_in[it, g, j].astype(F32)
        return total

    def gather(it, g, spec):
        ag[it, g, me_r] = spec.astype(BF16)
        for to in [to for h, to in rcv_at if h == 0 or g in GATHER_STRAIGHT]:
            pltpu.make_async_remote_copy(
                src_ref=ag.at[it, g, me_r], dst_ref=ag.at[it, g, me_r],
                send_sem=ag_send.at[it, g], recv_sem=ag_recv.at[it, g],
                device_id=(me_f, to), device_id_type=MESH,
            ).start()

    def relay(it, g):
        if nz > 1:
            wait(ag.at[it, g, pl.ds(0, nz - 1)], ag_recv.at[it, g])
        pltpu.make_async_remote_copy(
            src_ref=ag.at[it, g, ours], dst_ref=ag.at[it, g, ours],
            send_sem=relay_send.at[it, g], recv_sem=relay_recv.at[it, g],
            device_id=(me_f, mate), device_id_type=MESH,
        ).start()

    def adjoint(it, groups):
        for g in groups:
            if g in GATHER_STRAIGHT:
                wait(ag.at[it, g, pl.ds(0, nr - 1)], ag_recv.at[it, g])
            else:
                wait(ag.at[it, g, pl.ds(0, nz)], relay_recv.at[it, g])
        left = jnp.concatenate(
            [jnp.concatenate([ag[it, g, j] for j in range(nr)], axis=1) for g in groups], axis=0
        )
        one, two = [dot(left, jnp.concatenate([refl[0, w], refl[1, w]], axis=1)) for w in range(2)]
        lines = second[:deep * len(groups)]
        by_re = jnp.where(lines, two[:, :BX], one[:, :BX])
        by_im = jnp.where(lines, two[:, BX:], one[:, BX:])
        return by_re - turn(by_im)

    loads[0].wait()
    loads[1].wait()
    high, low = split(wave[...])
    both = dot_nt(to_bins[...], high)
    first[...] = both[:rows] + both[rows:] + dot_nt(to_bins[:rows], low)
    loads[2].wait()
    loads[4].wait()
    onset = onset_ref[...]
    early = lax.broadcasted_iota(jnp.int32, (NT, BX), 0) < onset
    onset_col = jnp.broadcast_to(onset, (BX, BX)).T

    def finish(spec):
        both = jnp.concatenate([spec.T, spec.T], axis=1).astype(BF16)
        field = dot(both, to_bins[...]) * (2.0 / NT)
        samples = lax.broadcasted_iota(jnp.int32, (BX, BX), 1)
        return [
            jnp.where(samples + k * BX < onset_col, field[:, k * BX:(k + 1) * BX], 0.0)
            for k in range(NT // BX)
        ]

    pl.semaphore_wait(barrier, nf + nr - 2)
    to_bin_owners(0, 0, first[...])
    loads[3].wait()
    for w in range(2):
        for c in range(2):
            for k in range(nr):
                block = refl[c, w, pl.ds(k * BX, BX), :]
                turned_refl[pl.ds((2 * w + c) * BX, BX), pl.ds(k * BX, BX)] = block.T
    for it in range(ITERS):
        for g in range(GROUPS):
            forward(it, g, from_time_owners(it, 0, g))
        for g in range(GROUPS):
            if g not in SUM_STRAIGHT:
                paired(it, g)
        for g in SUM_ORDER:
            to_time_owners(it, 0, g, summed(it, g))
        upward = from_bin_owners(it, 0)
        to_bin_owners(it, 1, spectrum(trace(upward)))
        if it == ITERS - 1:
            for k, part in enumerate(finish(upward.astype(F32))):
                minus_ref[0, :, pl.ds(k * BX, BX)] = part
        for g in range(GROUPS):
            gather(it, g, from_time_owners(it, 1, g))
        for g in range(GROUPS):
            if g not in GATHER_STRAIGHT:
                relay(it, g)
        for groups in GATHER_SETS:
            values = adjoint(it, groups)
            for k in range(len(groups) - 1, -1, -1):
                to_time_owners(it, 1, groups[k], values[k * deep:(k + 1) * deep])
        downward = from_bin_owners(it, 1)
        if it < ITERS - 1:
            to_bin_owners(it + 1, 0, first[...] + spectrum(trace(downward)))
        else:
            for k, part in enumerate(finish(downward.astype(F32))):
                span = pl.ds(k * BX, BX)
                plus_ref[0, :, span] = wave[:, span] + part

    for it in range(ITERS):
        for part in range(2):
            stage = 4 * it + 2 * part
            wait(a2a_out.at[stage, pl.ds(0, nf - 1)], bins_send.at[it, part])
            wait(a2a_out.at[stage + 1, pl.ds(0, nf - 1)], time_send.at[it, part])
        for g in range(GROUPS):
            if g in SUM_STRAIGHT:
                wait(rs_out.at[it, g, pl.ds(0, nr - 1)], rs_send.at[it, g])
            else:
                wait(rs_out.at[it, g, theirs], mate_send.at[it, g])
                if nz > 1:
                    wait(rs_pair.at[it, g, pl.ds(0, nz - 1)], rs_send.at[it, g])
            if g in GATHER_STRAIGHT:
                wait(ag.at[it, g, pl.ds(0, nr - 1)], ag_send.at[it, g])
            else:
                wait(ag.at[it, g, ours], relay_send.at[it, g])
                if nz > 1:
                    wait(ag.at[it, g, pl.ds(0, nz - 1)], ag_send.at[it, g])


def put(plus_ref, minus_ref, plus_out, minus_out, sems):
    copies = [
        pltpu.make_async_copy(plus_ref, plus_out, sems.at[0]),
        pltpu.make_async_copy(minus_ref, minus_out, sems.at[1]),
    ]
    for copy in copies:
        copy.start()
    for copy in copies:
        copy.wait()


def solution(mesh):
    nf, nr = mesh.shape["freq"], mesh.shape["rcv"]
    rows, deep = 4 * nf, 4 * nf // GROUPS
    to_bins, to_time = tables(2 * nf)

    def shards(direct_wave, reflection, onset):
        out = pltpu.VMEM(direct_wave.shape, F32)
        in_hbm = [
            pltpu.with_memory_space_constraint(array, pltpu.HBM)
            for array in (direct_wave, reflection, onset, jnp.asarray(to_bins), jnp.asarray(to_time))
        ]
        anywhere = pl.BlockSpec(memory_space=pl.ANY)
        vmem = pl.BlockSpec(memory_space=pltpu.VMEM)
        dma = pltpu.SemaphoreType.DMA
        plus, minus = pl.pallas_call(
            functools.partial(kernel, nf, nr),
            out_shape=(out, out),
            in_specs=[anywhere] * 5,
            out_specs=(vmem, vmem),
            scratch_shapes=[
                pltpu.VMEM(direct_wave.shape[1:], F32),
                pltpu.VMEM(reflection.shape, BF16),
                pltpu.VMEM(onset.shape, jnp.int32),
                pltpu.VMEM((4 * BX, nr * BX), BF16),
                pltpu.VMEM(to_bins.shape, BF16),
                pltpu.VMEM(to_time.shape, BF16),
                pltpu.VMEM((rows, BX), F32),
                pltpu.VMEM((4 * ITERS, nf, 4, BX), F32),
                pltpu.VMEM((4 * ITERS, nf, 4, BX), F32),
                pltpu.VMEM((ITERS, GROUPS, nr, deep, BX), BF16),
                pltpu.VMEM((ITERS, GROUPS, nr // 2, deep, BX), BF16),
                pltpu.VMEM((ITERS, GROUPS, nr // 2, deep, BX), BF16),
                pltpu.VMEM((ITERS, GROUPS, nr - 1, deep, BX), BF16),
                pltpu.VMEM((ITERS, GROUPS, nr, deep, BX), BF16),
                dma((5,)),
                dma((ITERS, 2)),
                dma((ITERS, 2, GROUPS)),
                dma((ITERS, 2)),
                dma((ITERS, 2)),
            ]
            + [dma((ITERS, GROUPS))] * 8,
            compiler_params=pltpu.CompilerParams(
                collective_id=0, has_side_effects=True, vmem_limit_bytes=32 * 2**20
            ),
        )(*in_hbm)
        shape = jax.ShapeDtypeStruct(direct_wave.shape, F32)
        return pl.pallas_call(
            put,
            out_shape=(shape, shape),
            in_specs=[vmem, vmem],
            out_specs=(anywhere, anywhere),
            scratch_shapes=[dma((2,))],
            compiler_params=pltpu.CompilerParams(vmem_limit_bytes=2**20),
        )(plus, minus)

    return jax.shard_map(
        shards,
        mesh=mesh,
        in_specs=(P("freq", "rcv", None), P(None, "freq", None, "rcv"), P("freq", "rcv")),
        out_specs=(P("freq", "rcv", None), P("freq", "rcv", None)),
        check_vma=False,
    )
```

```python
import functools
import math

import jax
import jax.numpy as jnp
import ml_dtypes
import numpy as np
from jax import lax
from jax.experimental import pallas as pl
from jax.experimental.pallas import tpu as pltpu
from jax.sharding import PartitionSpec as P

NT = 512
ITERS = 2
BX = 128
GROUPS = 4
SUM_STRAIGHT = (0, 3)
GATHER_STRAIGHT = (3,)
SUM_ORDER = (0, 3, 1, 2)
GATHER_SETS = ((3,), (0, 1, 2))
F32 = jnp.float32
BF16 = jnp.bfloat16
MESH = pl.DeviceIdType.MESH


def tables(bins):
    phase = np.outer(np.arange(1, bins + 1), np.arange(NT)) % NT
    angle = phase.astype(np.float64) * (2.0 * math.pi / NT)
    rows = np.stack([np.cos(angle), -np.sin(angle)], axis=1).reshape(2 * bins, NT)
    high = rows.astype(ml_dtypes.bfloat16)
    low = (rows - high.astype(np.float64)).astype(ml_dtypes.bfloat16)
    to_bins = np.concatenate([high, low], axis=0)
    scale = ml_dtypes.bfloat16(2.0 / NT)
    to_time = np.concatenate([high.T * scale, low.T * scale], axis=1)
    return to_bins, to_time.astype(ml_dtypes.bfloat16)


def dot(a, b):
    return jnp.dot(a, b, preferred_element_type=F32)


def dot_nt(a, b):
    return lax.dot_general(a, b, (((1,), (1,)), ((), ())), preferred_element_type=F32)


def split(x):
    high = x.astype(BF16)
    return high, (x - high.astype(F32)).astype(BF16)


def ring(n, k):
    return min(k % n, -k % n)


def offsets_freq(ny):
    steps = [(h, y, c) for h in range(2) for y in range(ny) for c in range(2)]
    return sorted(steps, key=lambda s: (ring(ny, s[1]) + 2 * s[0], -s[0], s[1], s[2]))


def offsets_rcv(nz):
    steps = [(h, z) for h in range(2) for z in range(nz)][1:]
    return sorted(steps, key=lambda s: (-ring(nz, s[1]) - s[0], s))


def kernel(
    nf, nr,
    wave_hbm, refl_hbm, onset_hbm, bins_hbm, time_hbm,
    plus_ref, minus_ref,
    wave, refl, onset_ref, turned_refl, to_bins, to_time, first,
    a2a_out, a2a_in, rs_out, rs_mate, rs_pair, rs_in, ag,
    load_sem, bins_send, bins_recv, time_send, time_recv, rs_send, rs_recv, ag_send, ag_recv,
    mate_send, mate_recv, relay_send, relay_recv,
):
    me_f = lax.axis_index("freq")
    me_r = lax.axis_index("rcv")
    rows = 4 * nf
    ny, nz = nf // 4, nr // 2
    near = offsets_freq(ny)
    back = [near.index((h, -y % ny, c)) for h, y, c in near]
    size = nf // GROUPS
    deep = 4 * size

    last = nf - max(size * GROUPS // 4, 1)
    issue_order = [*range(nf - 1, last - 1, -1), *range(1, last)]

    half, y_at, core = me_f // (2 * ny), (me_f // 2) % ny, me_f % 2
    freq_at = [
        (((half + h) % 2) * ny + (y_at + y) % ny) * 2 + (core + c) % 2 for h, y, c in near
    ]
    side, z_at = me_r // nz, me_r % nz
    rcv_at = [(h, (side + h) % 2 * nz + (z_at + z) % nz) for h, z in offsets_rcv(nz)]
    line_at = [to for h, to in rcv_at if h == 0]
    mate = (1 - side) * nz + z_at
    ours, theirs = pl.ds(side * nz, nz), pl.ds((1 - side) * nz, nz)

    loads = [
        pltpu.make_async_copy(src, dst, load_sem.at[i])
        for i, (src, dst) in enumerate(
            (
                (wave_hbm.at[0], wave), (bins_hbm, to_bins), (time_hbm, to_time),
                (refl_hbm, refl), (onset_hbm, onset_ref),
            )
        )
    ]
    for load in loads:
        load.start()

    barrier = pltpu.get_barrier_semaphore()
    peers = [(ring(ny, near[j][1]) + 2 * near[j][0], freq_at[j], me_r) for j in range(1, nf)]
    peers += [
        (ring(nz, z) + h, me_f, to) for (h, z), (_, to) in zip(offsets_rcv(nz), rcv_at)
    ]
    for _, f, r in sorted(peers, key=lambda peer: -peer[0]):
        pl.semaphore_signal(barrier, inc=1, device_id=(f, r), device_id_type=MESH)

    is_im = (lax.broadcasted_iota(jnp.int32, (rows, BX), 0) % 2) == 1
    second = ((lax.broadcasted_iota(jnp.int32, (rows, BX), 0) // 2) % 2) == 1
    group_second = second[:deep]
    def wait(ref, sem):
        pltpu.make_async_copy(ref, ref, sem).wait()

    def to_bin_owners(it, part, value):
        stage = 4 * it + 2 * part
        out, into = a2a_out.at[stage], a2a_in.at[stage]
        out[...] = value.reshape(nf, 4, BX)
        for j in issue_order:
            pltpu.make_async_remote_copy(
                src_ref=out.at[freq_at[j]], dst_ref=into.at[back[j]],
                send_sem=bins_send.at[it, part], recv_sem=bins_recv.at[it, part, back[j] // size],
                device_id=(freq_at[j], me_r), device_id_type=MESH,
            ).start()
        into[0] = out[me_f]

    def from_time_owners(it, part, g):
        stage, least = 4 * it + 2 * part, 1 if g == 0 else 0
        if size > least:
            wait(
                a2a_in.at[stage, pl.ds(g * size + least, size - least)], bins_recv.at[it, part, g]
            )
        return a2a_in[stage, pl.ds(g * size, size)].reshape(deep, BX)

    def to_time_owners(it, part, g, value):
        stage = 4 * it + 2 * part + 1
        out, into = a2a_out.at[stage], a2a_in.at[stage]
        out[pl.ds(g * size, size)] = value.reshape(size, 4, BX)
        for j in range((g + 1) * size - 1, max(g * size, 1) - 1, -1):
            pltpu.make_async_remote_copy(
                src_ref=out.at[j], dst_ref=into.at[me_f],
                send_sem=time_send.at[it, part], recv_sem=time_recv.at[it, part],
                device_id=(freq_at[j], me_r), device_id_type=MESH,
            ).start()
        if g == 0:
            into[me_f] = out[0]

    def from_bin_owners(it, part):
        stage = 4 * it + 2 * part + 1
        wait(a2a_in.at[stage, pl.ds(0, nf - 1)], time_recv.at[it, part])
        return a2a_in[stage].reshape(rows, BX).astype(BF16)

    def spectrum(field):
        both = dot(to_bins[...], field.astype(BF16))
        return both[:rows] + both[rows:]

    def trace(spec):
        both = jnp.concatenate([spec, spec], axis=0)
        return jnp.where(early, dot(to_time[...], both), 0.0)

    def turn(x):
        return jnp.where(is_im[:x.shape[0]], jnp.roll(x, 1, axis=0), -jnp.roll(x, -1, axis=0))

    def forward(it, g, spec):
        spec = spec.astype(BF16).astype(F32)
        turned = turn(spec)
        weights = jnp.concatenate(
            [
                jnp.where(group_second, 0.0, spec), jnp.where(group_second, 0.0, turned),
                jnp.where(group_second, spec, 0.0), jnp.where(group_second, turned, 0.0),
            ],
            axis=1,
        ).astype(BF16)
        for part in (1 - side, side):
            for k in range(nz // 2):
                at = part * nz + 2 * k
                columns = pl.ds(pl.multiple_of(at * BX, 2 * BX), 2 * BX)
                pair = dot(weights, turned_refl[:, columns]).astype(BF16)
                rs_out[it, g, at] = pair[:, :BX]
                rs_out[it, g, at + 1] = pair[:, BX:]
            if g in SUM_STRAIGHT:
                for j, (h, to) in enumerate(rcv_at):
                    if (h == 0) == (part is side):
                        pltpu.make_async_remote_copy(
                            src_ref=rs_out.at[it, g, to], dst_ref=rs_in.at[it, g, j],
                            send_sem=rs_send.at[it, g], recv_sem=rs_recv.at[it, g],
                            device_id=(me_f, to), device_id_type=MESH,
                        ).start()
            elif part is not side:
                pltpu.make_async_remote_copy(
                    src_ref=rs_out.at[it, g, theirs], dst_ref=rs_mate.at[it, g],
                    send_sem=mate_send.at[it, g], recv_sem=mate_recv.at[it, g],
                    device_id=(me_f, mate), device_id_type=MESH,
                ).start()

    def paired(it, g):
        wait(rs_mate.at[it, g], mate_recv.at[it, g])
        both = rs_out[it, g, ours].astype(F32) + rs_mate[it, g].astype(F32)
        rs_pair[it, g] = both.astype(BF16)
        for j, to in enumerate(line_at):
            pltpu.make_async_remote_copy(
                src_ref=rs_pair.at[it, g, to % nz], dst_ref=rs_in.at[it, g, j],
                send_sem=rs_send.at[it, g], recv_sem=rs_recv.at[it, g],
                device_id=(me_f, to), device_id_type=MESH,
            ).start()

    def summed(it, g):
        if g in SUM_STRAIGHT:
            terms, total = nr - 1, rs_out[it, g, me_r].astype(F32)
        else:
            terms, total = nz - 1, rs_pair[it, g, z_at].astype(F32)
        if terms:
            wait(rs_in.at[it, g, pl.ds(0, terms)], rs_recv.at[it, g])
        for j in range(terms):
            total = total + rs_in[it, g, j].astype(F32)
        return total

    def gather(it, g, spec):
        ag[it, g, me_r] = spec.astype(BF16)
        for to in [to for h, to in rcv_at if h == 0 or g in GATHER_STRAIGHT]:
            pltpu.make_async_remote_copy(
                src_ref=ag.at[it, g, me_r], dst_ref=ag.at[it, g, me_r],
                send_sem=ag_send.at[it, g], recv_sem=ag_recv.at[it, g],
                device_id=(me_f, to), device_id_type=MESH,
            ).start()

    def relay(it, g):
        if nz > 1:
            wait(ag.at[it, g, pl.ds(0, nz - 1)], ag_recv.at[it, g])
        pltpu.make_async_remote_copy(
            src_ref=ag.at[it, g, ours], dst_ref=ag.at[it, g, ours],
            send_sem=relay_send.at[it, g], recv_sem=relay_recv.at[it, g],
            device_id=(me_f, mate), device_id_type=MESH,
        ).start()

    def adjoint(it, groups):
        for g in groups:
            if g in GATHER_STRAIGHT:
                wait(ag.at[it, g, pl.ds(0, nr - 1)], ag_recv.at[it, g])
            else:
                wait(ag.at[it, g, pl.ds(0, nz)], relay_recv.at[it, g])
        left = jnp.concatenate(
            [jnp.concatenate([ag[it, g, j] for j in range(nr)], axis=1) for g in groups], axis=0
        )
        one, two = [dot(left, jnp.concatenate([refl[0, w], refl[1, w]], axis=1)) for w in range(2)]
        lines = second[:deep * len(groups)]
        by_re = jnp.where(lines, two[:, :BX], one[:, :BX])
        by_im = jnp.where(lines, two[:, BX:], one[:, BX:])
        return by_re - turn(by_im)

    loads[0].wait()
    loads[1].wait()
    high, low = split(wave[...])
    both = dot_nt(to_bins[...], high)
    first[...] = both[:rows] + both[rows:] + dot_nt(to_bins[:rows], low)
    loads[2].wait()
    loads[4].wait()
    onset = onset_ref[...]
    early = lax.broadcasted_iota(jnp.int32, (NT, BX), 0) < onset
    onset_col = jnp.broadcast_to(onset, (BX, BX)).T

    def finish(spec):
        both = jnp.concatenate([spec.T, spec.T], axis=1).astype(BF16)
        field = dot(both, to_bins[...]) * (2.0 / NT)
        samples = lax.broadcasted_iota(jnp.int32, (BX, BX), 1)
        return [
            jnp.where(samples + k * BX < onset_col, field[:, k * BX:(k + 1) * BX], 0.0)
            for k in range(NT // BX)
        ]

    pl.semaphore_wait(barrier, nf + nr - 2)
    to_bin_owners(0, 0, first[...])
    loads[3].wait()
    for w in range(2):
        for c in range(2):
            for k in range(nr):
                block = refl[c, w, pl.ds(k * BX, BX), :]
                turned_refl[pl.ds((2 * w + c) * BX, BX), pl.ds(k * BX, BX)] = block.T
    for it in range(ITERS):
        for g in range(GROUPS):
            forward(it, g, from_time_owners(it, 0, g))
        for g in range(GROUPS):
            if g not in SUM_STRAIGHT:
                paired(it, g)
        for g in SUM_ORDER:
            to_time_owners(it, 0, g, summed(it, g))
        upward = from_bin_owners(it, 0)
        to_bin_owners(it, 1, spectrum(trace(upward)))
        if it == ITERS - 1:
            for k, part in enumerate(finish(upward.astype(F32))):
                minus_ref[0, :, pl.ds(k * BX, BX)] = part
        for g in range(GROUPS):
            gather(it, g, from_time_owners(it, 1, g))
        for g in range(GROUPS):
            if g not in GATHER_STRAIGHT:
                relay(it, g)
        for groups in GATHER_SETS:
            values = adjoint(it, groups)
            for k in range(len(groups) - 1, -1, -1):
                to_time_owners(it, 1, groups[k], values[k * deep:(k + 1) * deep])
        downward = from_bin_owners(it, 1)
        if it < ITERS - 1:
            to_bin_owners(it + 1, 0, first[...] + spectrum(trace(downward)))
        else:
            for k, part in enumerate(finish(downward.astype(F32))):
                span = pl.ds(k * BX, BX)
                plus_ref[0, :, span] = wave[:, span] + part

    for it in range(ITERS):
        for part in range(2):
            stage = 4 * it + 2 * part
            wait(a2a_out.at[stage, pl.ds(0, nf - 1)], bins_send.at[it, part])
            wait(a2a_out.at[stage + 1, pl.ds(0, nf - 1)], time_send.at[it, part])
        for g in range(GROUPS):
            if g in SUM_STRAIGHT:
                wait(rs_out.at[it, g, pl.ds(0, nr - 1)], rs_send.at[it, g])
            else:
                wait(rs_out.at[it, g, theirs], mate_send.at[it, g])
                if nz > 1:
                    wait(rs_pair.at[it, g, pl.ds(0, nz - 1)], rs_send.at[it, g])
            if g in GATHER_STRAIGHT:
                wait(ag.at[it, g, pl.ds(0, nr - 1)], ag_send.at[it, g])
            else:
                wait(ag.at[it, g, ours], relay_send.at[it, g])
                if nz > 1:
                    wait(ag.at[it, g, pl.ds(0, nz - 1)], ag_send.at[it, g])


def put(plus_ref, minus_ref, plus_out, minus_out, sems):
    copies = [
        pltpu.make_async_copy(plus_ref, plus_out, sems.at[0]),
        pltpu.make_async_copy(minus_ref, minus_out, sems.at[1]),
    ]
    for copy in copies:
        copy.start()
    for copy in copies:
        copy.wait()


def solution(mesh):
    nf, nr = mesh.shape["freq"], mesh.shape["rcv"]
    rows, deep = 4 * nf, 4 * nf // GROUPS
    to_bins, to_time = tables(2 * nf)

    def shards(direct_wave, reflection, onset):
        out = pltpu.VMEM(direct_wave.shape, F32)
        in_hbm = [
            pltpu.with_memory_space_constraint(array, pltpu.HBM)
            for array in (direct_wave, reflection, onset, jnp.asarray(to_bins), jnp.asarray(to_time))
        ]
        anywhere = pl.BlockSpec(memory_space=pl.ANY)
        vmem = pl.BlockSpec(memory_space=pltpu.VMEM)
        dma = pltpu.SemaphoreType.DMA
        plus, minus = pl.pallas_call(
            functools.partial(kernel, nf, nr),
            out_shape=(out, out),
            in_specs=[anywhere] * 5,
            out_specs=(vmem, vmem),
            scratch_shapes=[
                pltpu.VMEM(direct_wave.shape[1:], F32),
                pltpu.VMEM(reflection.shape, BF16),
                pltpu.VMEM(onset.shape, jnp.int32),
                pltpu.VMEM((4 * BX, nr * BX), BF16),
                pltpu.VMEM(to_bins.shape, BF16),
                pltpu.VMEM(to_time.shape, BF16),
                pltpu.VMEM((rows, BX), F32),
                pltpu.VMEM((4 * ITERS, nf, 4, BX), F32),
                pltpu.VMEM((4 * ITERS, nf, 4, BX), F32),
                pltpu.VMEM((ITERS, GROUPS, nr, deep, BX), BF16),
                pltpu.VMEM((ITERS, GROUPS, nr // 2, deep, BX), BF16),
                pltpu.VMEM((ITERS, GROUPS, nr // 2, deep, BX), BF16),
                pltpu.VMEM((ITERS, GROUPS, nr - 1, deep, BX), BF16),
                pltpu.VMEM((ITERS, GROUPS, nr, deep, BX), BF16),
                dma((5,)),
                dma((ITERS, 2)),
                dma((ITERS, 2, GROUPS)),
                dma((ITERS, 2)),
                dma((ITERS, 2)),
            ]
            + [dma((ITERS, GROUPS))] * 8,
            compiler_params=pltpu.CompilerParams(
                collective_id=0, has_side_effects=True, vmem_limit_bytes=32 * 2**20
            ),
        )(*in_hbm)
        shape = jax.ShapeDtypeStruct(direct_wave.shape, F32)
        return pl.pallas_call(
            put,
            out_shape=(shape, shape),
            in_specs=[vmem, vmem],
            out_specs=(anywhere, anywhere),
            scratch_shapes=[dma((2,))],
            compiler_params=pltpu.CompilerParams(vmem_limit_bytes=2**20),
        )(plus, minus)

    return jax.shard_map(
        shards,
        mesh=mesh,
        in_specs=(P("freq", "rcv", None), P(None, "freq", None, "rcv"), P("freq", "rcv")),
        out_specs=(P("freq", "rcv", None), P("freq", "rcv", None)),
        check_vma=False,
    )
```
